256 devices in a mesh: dp: 32 (over z, x_hi, core), rep: 8 (over x_lo, y).
Axes of the slice: x: 4 (x_hi: 2, x_lo: 2; x = x_hi * 2 + x_lo), y: 4, z: 8, core: 2. Of those that a mesh axis runs over, the one named last changes fastest.
Arguments:
- image_student: float32 [8192, 512], P('dp'), may hold values from -12 to 12
- image_teacher: float32 [8192, 768], P('dp'), may hold values from -12 to 12
- text_features: float32 [8192, 512], P(('dp', 'rep')), may hold values from -12 to 12
- text_teacher: float32 [8192, 768], P(('dp', 'rep')), may hold values from -12 to 12
- head: float32 [512, 512], replicated, may hold values from -0.2 to 1.2
Outputs:
- grad_image: float32 [8192, 512], P('dp')
- grad_head: float32 [512, 512], replicated
The draws below stay inside these ranges and needn't reach their ends.
All inputs are finite; a program needn't handle non-finite values.
Results may differ from the reference program's by a relative error of at most 0.0004.
Values sent between devices are 32-bit elements; how exact they have to be, the bound alone decides.
No kernel may reach another device: no remote copies, remote signals or barrier semaphores. Data moves between devices by JAX's collectives and lax.ppermute only.
A program may use at most 64 MiB of HBM per device.

```python
import math
import jax
import jax.numpy as jnp
from jax import lax

DT = 768
DS = 512
ROWS = 256
BATCH = 8192
N_DP = 32


def paired_draw(key, count, width, every):
    key_query, key_key, key_noise = jax.random.split(key, 3)
    queries = jnp.clip(jax.random.normal(key_query, (count, width), jnp.float32), -6.0, 6.0)
    keys = jnp.clip(jax.random.normal(key_key, (count, width), jnp.float32), -6.0, 6.0)
    position = jnp.arange(count)
    chosen = (position % every == 5).astype(jnp.float32)
    target = (position * 97 + 3) % count
    level = 4.0 + 4.0 * (position % 3).astype(jnp.float32)
    signs = jnp.where(keys[target] >= 0.0, 1.0, -1.0)
    aligned = level[:, None] * signs
    queries = queries + chosen[:, None] * (aligned - queries)
    nearby = jnp.zeros((count,), jnp.float32).at[(target + 1) % count].max(chosen)
    noise = jnp.clip(jax.random.normal(key_noise, (count, width), jnp.float32), -6.0, 6.0)
    source = keys[(position - 1) % count]
    keys = keys + nearby[:, None] * (source + 0.1 * noise - keys)
    return (jnp.clip(queries, -12.0, 12.0), jnp.clip(keys, -12.0, 12.0))


def draw_image_teacher(key, part):
    every = 61
    queries, keys = paired_draw(key, BATCH, DT, every)
    return queries


def draw_text_teacher(key, part):
    every = 61
    queries, keys = paired_draw(key, BATCH, DT, every)
    return keys


def draw_image_student(key, part):
    every = 61
    queries, keys = paired_draw(jax.random.fold_in(key, 100), BATCH, DS, every)
    return queries


def draw_text_features(key, part):
    every = 61
    queries, keys = paired_draw(jax.random.fold_in(key, 100), BATCH, DS, every)
    return keys


def draw_head(key, part):
    key = jax.random.fold_in(key, 7)
    noise = jnp.clip(jax.random.normal(key, (DS, DS), jnp.float32), -2.0, 2.0)
    return jnp.eye(DS, dtype=jnp.float32) + 0.5 * noise / jnp.sqrt(jnp.float32(DS))


def setup_inputs(seed: int = 0) -> dict:
    arg_keys = jax.random.split(jax.random.key(seed), 6)
    return {
        "image_student": draw_image_student(jax.random.fold_in(arg_keys[5], 71), 0),
        "image_teacher": draw_image_teacher(jax.random.fold_in(arg_keys[5], 71), 0),
        "text_features": draw_text_features(jax.random.fold_in(arg_keys[5], 71), 0),
        "text_teacher": draw_text_teacher(jax.random.fold_in(arg_keys[5], 71), 0),
        "head": draw_head(jax.random.fold_in(arg_keys[5], 71), 0),
    }


def reference(image_student, image_teacher, text_features, text_teacher, head):
    highest = lax.Precision.HIGHEST
    scale_s = 4.0 / math.sqrt(DS)
    scale_t = 4.0 / math.sqrt(DT)
    text_student = jnp.dot(text_features, head, precision=highest, preferred_element_type=jnp.float32)
    blocks_s = image_student.reshape(N_DP, ROWS, DS)
    blocks_t = image_teacher.reshape(N_DP, ROWS, DT)

    def one_block(grad_text, pieces):
        queries_s, queries_t = pieces
        student = scale_s * jnp.dot(queries_s, text_student.T, precision=highest, preferred_element_type=jnp.float32)
        teacher = scale_t * jnp.dot(queries_t, text_teacher.T, precision=highest, preferred_element_type=jnp.float32)
        lse_student = jax.nn.logsumexp(student, axis=1)
        lse_teacher = jax.nn.logsumexp(teacher, axis=1)
        gap = jnp.exp(student - lse_student[:, None]) - jnp.exp(teacher - lse_teacher[:, None])
        rows_grad = scale_s * jnp.dot(gap, text_student, precision=highest, preferred_element_type=jnp.float32)
        grad_text = grad_text + scale_s * jnp.dot(gap.T, queries_s, precision=highest, preferred_element_type=jnp.float32)
        return (grad_text, rows_grad)
    start = jnp.zeros((BATCH, DS), jnp.float32)
    grad_text, rows_grads = lax.scan(one_block, start, (blocks_s, blocks_t))
    grad_image = rows_grads.reshape(BATCH, DS)
    grad_head = jnp.dot(text_features.T, grad_text, precision=highest, preferred_element_type=jnp.float32) / math.sqrt(BATCH)
    return (grad_image, grad_head)
```

```python
import math

import jax
import jax.numpy as jnp
from jax import lax
from jax.sharding import Mesh, PartitionSpec as P

AXES = ("z", "xh", "core", "xl", "y")
SIZES = (8, 2, 2, 2, 4)
HIGH = lax.Precision.HIGH


def linear(z, xh, core, xl, y):
    return (((z * 2 + xh) * 2 + core) * 2 + xl) * 4 + y


def moves(place):
    pairs = []
    for z in range(8):
        for xh in range(2):
            for core in range(2):
                for xl in range(2):
                    for y in range(4):
                        here = (z, xh, core, xl, y)
                        pairs.append((linear(*here), linear(*place(*here))))
    return pairs


Z_UP = moves(lambda z, xh, core, xl, y: ((z + 1) % 8, xh, core, xl, y))
Z_DOWN = moves(lambda z, xh, core, xl, y: ((z + 7) % 8, xh, core, xl, y))
X_FLIP = moves(lambda z, xh, core, xl, y: (z, 1 - xh, core, 1 - xl, y))
X_FAR = moves(lambda z, xh, core, xl, y: (z, 1 - xh, core, xl, y))
CORE = moves(lambda z, xh, core, xl, y: (z, xh, 1 - core, xl, y))
Z_FOLD = tuple(
    moves(lambda z, xh, core, xl, y, bit=bit: (z ^ bit, xh, core, xl, y)) for bit in (1, 2, 4)
)


def move(array, pairs):
    return lax.ppermute(array, AXES, pairs)


def dot(a, b, dims):
    return lax.dot_general(
        a, b, (dims, ((), ())), precision=HIGH, preferred_element_type=jnp.float32
    )


def part(folded, images, texts, width):
    features = texts[:, :width]
    student = dot(folded, features, ((1,), (1,)))
    teacher = dot(images, texts[:, width:], ((1,), (1,)))
    outs = []
    for tile in (student, teacher):
        top = jnp.max(tile, axis=1, keepdims=True)
        weight = jnp.exp(tile - top)
        total = jnp.sum(weight, axis=1, keepdims=True)
        outs.append((top, total, dot(weight, features, ((1,), (0,)))))
    return outs


def merged(first, second):
    top = jnp.maximum(first[0], second[0])
    a = jnp.exp(first[0] - top)
    b = jnp.exp(second[0] - top)
    return (top, first[1] * a + second[1] * b, first[2] * a + second[2] * b)


def shards(image_student, image_teacher, text_features, text_teacher, head):
    rows, width = image_student.shape
    scale_s = 4.0 / math.sqrt(width)
    scale_t = 4.0 / math.sqrt(image_teacher.shape[1])
    batch = rows * 32
    folded = scale_s * dot(image_student, head, ((1,), (1,)))
    images = scale_t * image_teacher

    own = jnp.concatenate([text_features, text_teacher], axis=1)
    up, down = move(own, Z_UP), move(own, Z_DOWN)
    group1 = jnp.concatenate([own, up, down], axis=0)
    up, down = move(up, Z_UP), move(down, Z_DOWN)
    across1 = move(group1, X_FLIP)
    group2 = jnp.concatenate([up, down], axis=0)
    up, down = move(up, Z_UP), move(down, Z_DOWN)
    across2 = move(group2, X_FLIP)
    group3 = jnp.concatenate([up, down], axis=0)
    up = move(up, Z_UP)
    across3 = move(group3, X_FLIP)
    across4 = move(up, X_FLIP)
    early = [group1, group2, across1]
    late = [group3, up, across2]
    last = [across3, across4]
    state = None
    for blocks in (early, late, last):
        texts = jnp.concatenate(blocks + [move(block, CORE) for block in blocks], axis=0)
        fresh = part(folded, images, texts, width)
        state = fresh if state is None else [merged(a, b) for a, b in zip(state, fresh)]
    (top_s, sum_s, prod_s), (top_t, sum_t, prod_t) = state

    columns = width // 8
    both = jnp.concatenate(
        [prod_s.reshape(rows, 8, columns), prod_t.reshape(rows, 8, columns)], axis=2
    ).transpose(1, 0, 2)
    stats = jnp.concatenate([top_s, sum_s, top_t, sum_t], axis=1).T.reshape(8, 128)
    both = jnp.concatenate([both, jnp.broadcast_to(stats[None], (8, 8, 128))], axis=1)
    both = lax.all_to_all(both, ("xl", "y"), 0, 0, tiled=True)
    stats = both[:, rows:, :].reshape(8, 4, rows)
    both = both[:, :rows, :]
    factors = []
    for k in (0, 2):
        tops = stats[:, k]
        top = jnp.max(tops, axis=0)
        shares = jnp.exp(tops - top[None])
        total = jnp.sum(shares * stats[:, k + 1], axis=0)
        factors.append(shares / total[None])
    summed_s = jnp.sum(both[:, :, :columns] * factors[0][:, :, None], axis=0)
    summed_t = jnp.sum(both[:, :, columns:] * factors[1][:, :, None], axis=0)
    gap_text = summed_s - summed_t

    term = dot(gap_text, image_student, ((0,), (0,)))
    core = lax.axis_index("core")
    half = columns // 2
    mine = lax.dynamic_slice_in_dim(term, core * half, half, 0)
    other = lax.dynamic_slice_in_dim(term, (1 - core) * half, half, 0)
    term = mine + move(other, CORE)
    for pairs in Z_FOLD + (X_FAR,):
        term = term + move(term, pairs)

    payload = jnp.concatenate(
        [
            jnp.concatenate([gap_text[: rows // 2], gap_text[rows // 2 :]], axis=1),
            term.reshape(half, 4, 128).transpose(1, 0, 2).reshape(4 * half, 128),
        ],
        axis=0,
    )
    payload = lax.all_to_all(
        jnp.broadcast_to(payload[None], (8,) + payload.shape), ("xl", "y"), 0, 0, tiled=True
    )
    gap_text = payload[:, : rows // 2].reshape(8, rows // 2, 2, columns)
    gap_text = gap_text.transpose(2, 1, 0, 3).reshape(rows, width)
    grad_image = scale_s * dot(gap_text, head, ((1,), (0,)))
    term = payload[:, rows // 2 :].reshape(8, 4, half, 128).transpose(0, 2, 1, 3).reshape(8, half, width)
    partner = move(term, CORE)
    low = jnp.where(core == 0, term, partner)
    high = jnp.where(core == 0, partner, term)
    grad_head = jnp.stack([low, high], axis=1).reshape(width, width)
    return (grad_image, grad_head * (scale_s / math.sqrt(batch)))


def solution(mesh):
    fine = Mesh(mesh.devices.reshape(SIZES), AXES)
    dp, every = ("z", "xh", "core"), AXES
    in_specs = (P(dp, None), P(dp, None), P(every, None), P(every, None), P())
    out_specs = (P(dp, None), P())
    return jax.shard_map(shards, mesh=fine, in_specs=in_specs, out_specs=out_specs, check_vma=False)
```

```python
import math

import jax
import jax.numpy as jnp
from jax import lax
from jax.experimental import pallas as pl
from jax.experimental.pallas import tpu as pltpu
from jax.sharding import Mesh, PartitionSpec as P

AXES = ("z", "xh", "core", "xl", "y")
SIZES = (8, 2, 2, 2, 4)
HIGH = lax.Precision.HIGH
DS, DT = 512, 768
ROWS = 256
SHARD = 32
COLS = DS // 8
VMEM_LIMIT = 14 * 1024 * 1024


def linear(z, xh, core, xl, y):
    return (((z * 2 + xh) * 2 + core) * 2 + xl) * 4 + y


def moves(place):
    pairs = []
    for z in range(8):
        for xh in range(2):
            for core in range(2):
                for xl in range(2):
                    for y in range(4):
                        here = (z, xh, core, xl, y)
                        pairs.append((linear(*here), linear(*place(*here))))
    return pairs


Z_NEXT = moves(lambda z, xh, core, xl, y: ((z + 1 - 2 * core) % 8, xh, core, xl, y))
X_FLIP = moves(lambda z, xh, core, xl, y: (z, 1 - xh, core, 1 - xl, y))
CORE = moves(lambda z, xh, core, xl, y: (z, xh, 1 - core, xl, y))
Z_FOLD = tuple(
    moves(lambda z, xh, core, xl, y, bit=bit: (z ^ bit, xh, core, xl, y)) for bit in (1, 2, 4)
)


def move(array, pairs):
    return lax.ppermute(array, AXES, pairs)


def dot(a, b, dims):
    return lax.dot_general(
        a, b, (dims, ((), ())), precision=HIGH, preferred_element_type=jnp.float32
    )


def split(x):
    high = x.astype(jnp.bfloat16)
    return high, (x - high.astype(jnp.float32)).astype(jnp.bfloat16)


def dot3(a, b, dims):
    def one(p, q):
        return lax.dot_general(p, q, (dims, ((), ())), preferred_element_type=jnp.float32)

    return one(a[0], b[0]) + (one(a[0], b[1]) + one(a[1], b[0]))


NT = ((1,), (1,))
NN = ((1,), (0,))


def texts_kernel(count, first, last, *refs):
    refs = list(refs)
    place = refs.pop(0) if last else None
    folded_ref, images_ref = refs.pop(0), refs.pop(0)
    arrays = [refs.pop(0) for _ in range(count)]
    state = None if first else [refs.pop(0) for _ in range(3)]
    outs = [refs.pop(0) for _ in range(1 if last else 3)]
    t_high, t_low, f_high, f_low = refs
    start = 0
    for array in arrays:
        here = pl.ds(start, array.shape[0])
        start += array.shape[0]
        t_high[here, :], t_low[here, :] = split(array[:, :DT])
        f_high[here, :], f_low[here, :] = split(array[:, DT:])
    texts = (t_high[...], t_low[...])
    features = (f_high[...], f_low[...])
    tiles = (
        dot3(split(folded_ref[...]), features, NT),
        dot3(split(images_ref[...]), texts, NT),
    )
    lane = lax.broadcasted_iota(jnp.int32, (ROWS, 128), 1)
    stats = jnp.zeros((ROWS, 128), jnp.float32)
    products = []
    for k, tile in enumerate(tiles):
        top = jnp.max(tile, axis=1, keepdims=True)
        if not first:
            old_top = state[0][:, 2 * k : 2 * k + 1]
            top = jnp.maximum(top, old_top)
        weight = jnp.exp(tile - top)
        total = jnp.sum(weight, axis=1, keepdims=True)
        product = dot3(split(weight), features, NN)
        if not first:
            shrink = jnp.exp(old_top - top)
            total = total + shrink * state[0][:, 2 * k + 1 : 2 * k + 2]
            product = product + shrink * state[1 + k][...]
        stats = jnp.where(lane == 2 * k, top, stats)
        stats = jnp.where(lane == 2 * k + 1, total, stats)
        products.append(product)
    if not last:
        outs[0][...] = stats
        outs[1][...] = products[0]
        outs[2][...] = products[1]
        return
    out = outs[0]
    turned = stats.T[:8]
    for q in range(4):
        a = products[0][:, 128 * q : 128 * q + 128]
        b = products[1][:, 128 * q : 128 * q + 128]
        out[place[2 * q], 0:ROWS] = jnp.where(lane < COLS, a, pltpu.roll(b, COLS, 1))
        out[place[2 * q + 1], 0:ROWS] = jnp.where(lane < COLS, pltpu.roll(a, COLS, 1), b)
    for k in range(8):
        out[k, ROWS : ROWS + 8] = turned[:, :128]
        out[k, ROWS + 8 : ROWS + 16] = turned[:, 128:]


def add_texts(folded, images, arrays, state=None, place=None):
    first, last = state is None, place is not None
    texts = sum(array.shape[0] for array in arrays)
    operands = [folded, images] + list(arrays) + ([] if first else list(state))
    vmem = pl.BlockSpec(memory_space=pltpu.VMEM)
    in_specs = [vmem] * len(operands)
    scratch = [
        pltpu.VMEM((texts, DT), jnp.bfloat16),
        pltpu.VMEM((texts, DT), jnp.bfloat16),
        pltpu.VMEM((texts, DS), jnp.bfloat16),
        pltpu.VMEM((texts, DS), jnp.bfloat16),
    ]
    if last:
        operands = [place] + operands
        in_specs = [pl.BlockSpec(memory_space=pltpu.SMEM)] + in_specs
        shapes = [jax.ShapeDtypeStruct((8, ROWS + 16, 128), jnp.float32)]
    else:
        shapes = [
            jax.ShapeDtypeStruct((ROWS, 128), jnp.float32),
            jax.ShapeDtypeStruct((ROWS, DS), jnp.float32),
            jax.ShapeDtypeStruct((ROWS, DS), jnp.float32),
        ]
    flops = 2 * 3 * ROWS * texts * (DT + 3 * DS)

    def body(*refs):
        texts_kernel(len(arrays), first, last, *refs)

    return pl.pallas_call(
        body,
        out_shape=shapes,
        in_specs=in_specs,
        out_specs=[vmem] * len(shapes),
        scratch_shapes=scratch,
        compiler_params=pltpu.CompilerParams(vmem_limit_bytes=VMEM_LIMIT),
        cost_estimate=pl.CostEstimate(
            flops=40 * flops, bytes_accessed=4 * 1024 * 1024, transcendentals=2 * ROWS * texts
        ),
        name="add_texts",
    )(*operands)


def halved(array, index, pairs):
    rows = array.shape[0] // 2
    mine = lax.dynamic_slice_in_dim(array, index * rows, rows, 0)
    other = lax.dynamic_slice_in_dim(array, (1 - index) * rows, rows, 0)
    return mine + move(other, pairs)


def to_all(piece, axes):
    count = math.prod(lax.axis_size(axis) for axis in axes)
    pieces = jnp.broadcast_to(piece[None], (count,) + piece.shape)
    return lax.all_to_all(pieces, axes, 0, 0, tiled=True)


def shards(image_student, image_teacher, text_features, text_teacher, head):
    scale_s = 4.0 / math.sqrt(DS)
    scale_t = 4.0 / math.sqrt(DT)
    batch = ROWS * 32
    xh, core = lax.axis_index("xh"), lax.axis_index("core")
    folded = scale_s * dot(image_student, head, NT)
    images = scale_t * image_teacher

    own = jnp.concatenate([text_teacher, text_features], axis=1)
    across = [move(text_teacher, X_FLIP), move(text_features, X_FLIP)]
    one = jnp.concatenate([own, jnp.concatenate(across, axis=1)], axis=0)
    one, two = lax.optimization_barrier((one, move(one, CORE)))
    state = add_texts(folded, images, [one, two])
    for step in range(3):
        one, two = move(one, Z_NEXT), move(two, Z_NEXT)
        state = add_texts(folded, images, [one, move(one, CORE)], state)
        state = add_texts(folded, images, [two, move(two, CORE)], state)
    one = move(one, Z_NEXT)
    place = jnp.arange(8, dtype=jnp.int32) ^ (4 * xh).astype(jnp.int32)
    (both,) = add_texts(folded, images, [one, move(one, CORE)], state, place)

    got = lax.all_to_all(both, ("xl", "y"), 0, 0, tiled=True)
    stats = got[:, ROWS:].reshape(8, 2, 8, 128)[:, :, :4]
    stats = stats.transpose(0, 2, 1, 3).reshape(8, 4, ROWS)
    sums = []
    for k in (0, 2):
        tops = stats[:, k]
        top = jnp.max(tops, axis=0)
        shares = jnp.exp(tops - top[None])
        total = jnp.sum(shares * stats[:, k + 1], axis=0)
        shares = shares / total[None]
        lanes = slice(0, COLS) if k == 0 else slice(COLS, 2 * COLS)
        sums.append(jnp.sum(got[:, :ROWS, lanes] * shares[:, :, None], axis=0))
    gap_text = sums[0] - sums[1]

    term = dot(gap_text, image_student, ((0,), (0,)))
    term = halved(term, core, CORE)
    piece = jnp.concatenate([gap_text[: ROWS // 2], gap_text[ROWS // 2 :]], axis=1)
    term, piece = lax.optimization_barrier((term, piece))
    term = halved(term, xh, X_FLIP)
    for pairs in Z_FOLD:
        term = term + move(term, pairs)

    gaps = to_all(piece, ("xl", "y"))
    gaps = jnp.where(xh == 0, gaps, jnp.concatenate([gaps[4:], gaps[:4]], axis=0))
    gap_text = gaps.reshape(8, ROWS // 2, 2, COLS).transpose(2, 1, 0, 3).reshape(ROWS, DS)
    grad_image = scale_s * dot(gap_text, head, NN)

    terms = to_all(term * (scale_s / math.sqrt(batch)), ("xh", "xl", "y"))
    terms = terms.reshape(2, 2, 4, SHARD // 2, DS)
    terms = jnp.stack([terms[0], terms[1, ::-1]], axis=2).reshape(8, SHARD, DS)
    partner = move(terms, CORE)
    low = jnp.where(core == 0, terms, partner)
    high = jnp.where(core == 0, partner, terms)
    grad_head = jnp.stack([low, high], axis=1).reshape(DS, DS)
    return (grad_image, grad_head)


def solution(mesh):
    fine = Mesh(mesh.devices.reshape(SIZES), AXES)
    dp, every = ("z", "xh", "core"), AXES
    in_specs = (P(dp, None), P(dp, None), P(every, None), P(every, None), P())
    out_specs = (P(dp, None), P())
    return jax.shard_map(shards, mesh=fine, in_specs=in_specs, out_specs=out_specs, check_vma=False)
```

```python
import math

import jax
import jax.numpy as jnp
from jax import lax
from jax.experimental import pallas as pl
from jax.experimental.pallas import tpu as pltpu
from jax.sharding import Mesh, PartitionSpec as P

AXES = ("z", "xh", "core", "xl", "y")
SIZES = (8, 2, 2, 2, 4)
HIGH = lax.Precision.HIGH
DS, DT = 512, 768
ROWS = 256
SHARD = 32
COLS = DS // 8
VMEM_LIMIT = 14 * 1024 * 1024


def linear(z, xh, core, xl, y):
    return (((z * 2 + xh) * 2 + core) * 2 + xl) * 4 + y


def moves(place):
    pairs = []
    for z in range(8):
        for xh in range(2):
            for core in range(2):
                for xl in range(2):
                    for y in range(4):
                        here = (z, xh, core, xl, y)
                        pairs.append((linear(*here), linear(*place(*here))))
    return pairs


Z_NEXT = moves(lambda z, xh, core, xl, y: ((z + 1 - 2 * core) % 8, xh, core, xl, y))
X_FLIP = moves(lambda z, xh, core, xl, y: (z, 1 - xh, core, 1 - xl, y))
CORE = moves(lambda z, xh, core, xl, y: (z, xh, 1 - core, xl, y))
Z_FOLD = tuple(
    moves(lambda z, xh, core, xl, y, bit=bit: (z ^ bit, xh, core, xl, y)) for bit in (1, 2, 6)
)


def move(array, pairs):
    return lax.ppermute(array, AXES, pairs)


def dot(a, b, dims):
    return lax.dot_general(
        a, b, (dims, ((), ())), precision=HIGH, preferred_element_type=jnp.float32
    )


def split(x):
    high = x.astype(jnp.bfloat16)
    return high, (x - high.astype(jnp.float32)).astype(jnp.bfloat16)


def dot3(a, b, dims):
    def one(p, q):
        return lax.dot_general(p, q, (dims, ((), ())), preferred_element_type=jnp.float32)

    return one(a[0], b[0]) + (one(a[0], b[1]) + one(a[1], b[0]))


NT = ((1,), (1,))
NN = ((1,), (0,))


def texts_kernel(count, first, last, *refs):
    refs = list(refs)
    place = refs.pop(0) if last else None
    folded_ref, images_ref = refs.pop(0), refs.pop(0)
    arrays = [refs.pop(0) for _ in range(count)]
    state = None if first else [refs.pop(0) for _ in range(3)]
    outs = [refs.pop(0) for _ in range(1 if last else 3)]
    t_high, t_low, f_high, f_low = refs
    start = 0
    for array in arrays:
        here = pl.ds(start, array.shape[0])
        start += array.shape[0]
        t_high[here, :], t_low[here, :] = split(array[:, :DT])
        f_high[here, :], f_low[here, :] = split(array[:, DT:])
    texts = (t_high[...], t_low[...])
    features = (f_high[...], f_low[...])
    tiles = (
        dot3(split(folded_ref[...]), features, NT),
        dot3(split(images_ref[...]), texts, NT),
    )
    lane = lax.broadcasted_iota(jnp.int32, (ROWS, 128), 1)
    stats = jnp.zeros((ROWS, 128), jnp.float32)
    products = []
    for k, tile in enumerate(tiles):
        top = jnp.max(tile, axis=1, keepdims=True)
        if not first:
            old_top = state[0][:, 2 * k : 2 * k + 1]
            top = jnp.maximum(top, old_top)
        weight = jnp.exp(tile - top)
        total = jnp.sum(weight, axis=1, keepdims=True)
        product = dot3(split(weight), features, NN)
        if not first:
            shrink = jnp.exp(old_top - top)
            total = total + shrink * state[0][:, 2 * k + 1 : 2 * k + 2]
            product = product + shrink * state[1 + k][...]
        stats = jnp.where(lane == 2 * k, top, stats)
        stats = jnp.where(lane == 2 * k + 1, total, stats)
        products.append(product)
    if not last:
        outs[0][...] = stats
        outs[1][...] = products[0]
        outs[2][...] = products[1]
        return
    out = outs[0]
    turned = stats.T[:8]
    for q in range(4):
        a = products[0][:, 128 * q : 128 * q + 128]
        b = products[1][:, 128 * q : 128 * q + 128]
        out[place[2 * q], 0:ROWS] = jnp.where(lane < COLS, a, pltpu.roll(b, COLS, 1))
        out[place[2 * q + 1], 0:ROWS] = jnp.where(lane < COLS, pltpu.roll(a, COLS, 1), b)
    for k in range(8):
        out[k, ROWS : ROWS + 8] = turned[:, :128]
        out[k, ROWS + 8 : ROWS + 16] = turned[:, 128:]


def add_texts(folded, images, arrays, state=None, place=None):
    first, last = state is None, place is not None
    texts = sum(array.shape[0] for array in arrays)
    operands = [folded, images] + list(arrays) + ([] if first else list(state))
    vmem = pl.BlockSpec(memory_space=pltpu.VMEM)
    in_specs = [vmem] * len(operands)
    scratch = [
        pltpu.VMEM((texts, DT), jnp.bfloat16),
        pltpu.VMEM((texts, DT), jnp.bfloat16),
        pltpu.VMEM((texts, DS), jnp.bfloat16),
        pltpu.VMEM((texts, DS), jnp.bfloat16),
    ]
    if last:
        operands = [place] + operands
        in_specs = [pl.BlockSpec(memory_space=pltpu.SMEM)] + in_specs
        shapes = [jax.ShapeDtypeStruct((8, ROWS + 16, 128), jnp.float32)]
    else:
        shapes = [
            jax.ShapeDtypeStruct((ROWS, 128), jnp.float32),
            jax.ShapeDtypeStruct((ROWS, DS), jnp.float32),
            jax.ShapeDtypeStruct((ROWS, DS), jnp.float32),
        ]
    flops = 2 * 3 * ROWS * texts * (DT + 3 * DS)

    def body(*refs):
        texts_kernel(len(arrays), first, last, *refs)

    return pl.pallas_call(
        body,
        out_shape=shapes,
        in_specs=in_specs,
        out_specs=[vmem] * len(shapes),
        scratch_shapes=scratch,
        compiler_params=pltpu.CompilerParams(vmem_limit_bytes=VMEM_LIMIT),
        cost_estimate=pl.CostEstimate(
            flops=40 * flops, bytes_accessed=4 * 1024 * 1024, transcendentals=2 * ROWS * texts
        ),
        name="add_texts",
    )(*operands)


def halved(array, index, pairs):
    rows = array.shape[0] // 2
    mine = lax.dynamic_slice_in_dim(array, index * rows, rows, 0)
    other = lax.dynamic_slice_in_dim(array, (1 - index) * rows, rows, 0)
    return mine + move(other, pairs)


def to_all(piece, axes):
    count = math.prod(lax.axis_size(axis) for axis in axes)
    pieces = jnp.broadcast_to(piece[None], (count,) + piece.shape)
    return lax.all_to_all(pieces, axes, 0, 0, tiled=True)


def shards(image_student, image_teacher, text_features, text_teacher, head):
    scale_s = 4.0 / math.sqrt(DS)
    scale_t = 4.0 / math.sqrt(DT)
    batch = ROWS * 32
    xh, core = lax.axis_index("xh"), lax.axis_index("core")
    folded = scale_s * dot(image_student, head, NT)
    images = scale_t * image_teacher

    own = [text_teacher, text_features]
    near = [move(array, CORE) for array in own]
    far = [move(array, X_FLIP) for array in own]
    one = jnp.concatenate([jnp.concatenate(part, axis=1) for part in (own, near)], axis=0)
    *far, _ = lax.optimization_barrier((*far, one))
    last = [move(array, CORE) for array in far]
    two = jnp.concatenate([jnp.concatenate(part, axis=1) for part in (far, last)], axis=0)
    state = add_texts(folded, images, [one, two])
    for step in range(3):
        one, two = move(one, Z_NEXT), move(two, Z_NEXT)
        state = add_texts(folded, images, [one, move(one, CORE)], state)
        state = add_texts(folded, images, [two, move(two, CORE)], state)
    one, two = move(one[:SHARD], Z_NEXT), move(two[:SHARD], Z_NEXT)
    two, *state = lax.optimization_barrier((two, *state))
    state = add_texts(folded, images, [one, move(one, CORE)], state)
    place = jnp.arange(8, dtype=jnp.int32) ^ (4 * xh).astype(jnp.int32)
    (both,) = add_texts(folded, images, [two, move(two, CORE)], state, place)

    got = lax.all_to_all(both, ("xl", "y"), 0, 0, tiled=True)
    stats = got[:, ROWS:].reshape(8, 2, 8, 128)[:, :, :4]
    stats = stats.transpose(0, 2, 1, 3).reshape(8, 4, ROWS)
    sums = []
    for k in (0, 2):
        tops = stats[:, k]
        top = jnp.max(tops, axis=0)
        shares = jnp.exp(tops - top[None])
        total = jnp.sum(shares * stats[:, k + 1], axis=0)
        shares = shares / total[None]
        lanes = slice(0, COLS) if k == 0 else slice(COLS, 2 * COLS)
        sums.append(jnp.sum(got[:, :ROWS, lanes] * shares[:, :, None], axis=0))
    gap_text = sums[0] - sums[1]

    term = dot(gap_text, image_student, ((0,), (0,)))
    term = halved(term, core, CORE)
    piece = jnp.concatenate([gap_text[: ROWS // 2], gap_text[ROWS // 2 :]], axis=1)
    term, piece = lax.optimization_barrier((term, piece))
    term = halved(term, xh, X_FLIP)
    for pairs in Z_FOLD:
        term = term + move(term, pairs)

    gaps = to_all(piece, ("xl", "y"))
    gaps = jnp.where(xh == 0, gaps, jnp.concatenate([gaps[4:], gaps[:4]], axis=0))
    gap_text = gaps.reshape(8, ROWS // 2, 2, COLS).transpose(2, 1, 0, 3).reshape(ROWS, DS)
    grad_image = scale_s * dot(gap_text, head, NN)

    terms = to_all(term * (scale_s / math.sqrt(batch)), ("xh", "xl", "y"))
    terms = terms.reshape(2, 2, 4, SHARD // 2, DS)
    terms = jnp.stack([terms[0], terms[1, ::-1]], axis=2).reshape(8, SHARD, DS)
    partner = move(terms, CORE)
    low = jnp.where(core == 0, terms, partner)
    high = jnp.where(core == 0, partner, terms)
    grad_head = jnp.stack([low, high], axis=1).reshape(DS, DS)
    return (grad_image, grad_head)


def solution(mesh):
    fine = Mesh(mesh.devices.reshape(SIZES), AXES)
    dp, every = ("z", "xh", "core"), AXES
    in_specs = (P(dp, None), P(dp, None), P(every, None), P(every, None), P())
    out_specs = (P(dp, None), P())
    return jax.shard_map(shards, mesh=fine, in_specs=in_specs, out_specs=out_specs, check_vma=False)
```

```python
import math

import jax
import jax.numpy as jnp
from jax import lax
from jax.experimental import pallas as pl
from jax.experimental.pallas import tpu as pltpu
from jax.sharding import Mesh, PartitionSpec as P

AXES = ("z", "xh", "core", "xl", "y")
SIZES = (8, 2, 2, 2, 4)
HIGH = lax.Precision.HIGH
DS, DT = 512, 768
ROWS = 256
SHARD = 32
COLS = DS // 8
VMEM_LIMIT = 14 * 1024 * 1024


def linear(z, xh, core, xl, y):
    return (((z * 2 + xh) * 2 + core) * 2 + xl) * 4 + y


def moves(place):
    pairs = []
    for z in range(8):
        for xh in range(2):
            for core in range(2):
                for xl in range(2):
                    for y in range(4):
                        here = (z, xh, core, xl, y)
                        pairs.append((linear(*here), linear(*place(*here))))
    return pairs


Z_NEXT = moves(lambda z, xh, core, xl, y: ((z + 1 - 2 * core) % 8, xh, core, xl, y))
X_FLIP = moves(lambda z, xh, core, xl, y: (z, 1 - xh, core, 1 - xl, y))
CORE = moves(lambda z, xh, core, xl, y: (z, xh, 1 - core, xl, y))
Z_FOLD = tuple(
    moves(lambda z, xh, core, xl, y, bit=bit: (z ^ bit, xh, core, xl, y)) for bit in (1, 2, 6)
)


def move(array, pairs):
    return lax.ppermute(array, AXES, pairs)


def dot(a, b, dims):
    return lax.dot_general(
        a, b, (dims, ((), ())), precision=HIGH, preferred_element_type=jnp.float32
    )


def split(x):
    high = x.astype(jnp.bfloat16)
    return high, (x - high.astype(jnp.float32)).astype(jnp.bfloat16)


def dot3(a, b, dims):
    def one(p, q):
        return lax.dot_general(p, q, (dims, ((), ())), preferred_element_type=jnp.float32)

    return one(a[0], b[0]) + (one(a[0], b[1]) + one(a[1], b[0]))


NT = ((1,), (1,))
NN = ((1,), (0,))


def texts_kernel(count, first, last, *refs):
    refs = list(refs)
    place = refs.pop(0) if last else None
    folded_ref, images_ref = refs.pop(0), refs.pop(0)
    arrays = [refs.pop(0) for _ in range(count)]
    state = None if first else [refs.pop(0) for _ in range(3)]
    outs = [refs.pop(0) for _ in range(1 if last else 3)]
    t_high, t_low, f_high, f_low = refs
    start = 0
    for array in arrays:
        here = pl.ds(start, array.shape[0])
        start += array.shape[0]
        t_high[here, :], t_low[here, :] = split(array[:, :DT])
        f_high[here, :], f_low[here, :] = split(array[:, DT:])
    texts = (t_high[...], t_low[...])
    features = (f_high[...], f_low[...])
    tiles = (
        dot3(split(folded_ref[...]), features, NT),
        dot3(split(images_ref[...]), texts, NT),
    )
    lane = lax.broadcasted_iota(jnp.int32, (ROWS, 128), 1)
    stats = jnp.zeros((ROWS, 128), jnp.float32)
    products = []
    for k, tile in enumerate(tiles):
        top = jnp.max(tile, axis=1, keepdims=True)
        if not first:
            old_top = state[0][:, 2 * k : 2 * k + 1]
            top = jnp.maximum(top, old_top)
        weight = jnp.exp(tile - top)
        total = jnp.sum(weight, axis=1, keepdims=True)
        product = dot3(split(weight), features, NN)
        if not first:
            shrink = jnp.exp(old_top - top)
            total = total + shrink * state[0][:, 2 * k + 1 : 2 * k + 2]
            product = product + shrink * state[1 + k][...]
        stats = jnp.where(lane == 2 * k, top, stats)
        stats = jnp.where(lane == 2 * k + 1, total, stats)
        products.append(product)
    if not last:
        outs[0][...] = stats
        outs[1][...] = products[0]
        outs[2][...] = products[1]
        return
    out = outs[0]
    turned = stats.T[:8]
    for q in range(4):
        a = products[0][:, 128 * q : 128 * q + 128]
        b = products[1][:, 128 * q : 128 * q + 128]
        out[place[2 * q], 0:ROWS] = jnp.where(lane < COLS, a, pltpu.roll(b, COLS, 1))
        out[place[2 * q + 1], 0:ROWS] = jnp.where(lane < COLS, pltpu.roll(a, COLS, 1), b)
    for k in range(8):
        out[k, ROWS : ROWS + 4] = turned[:4, :128]
        out[k, ROWS + 4 : ROWS + 8] = turned[:4, 128:]


def add_texts(folded, images, arrays, state=None, place=None):
    first, last = state is None, place is not None
    texts = sum(array.shape[0] for array in arrays)
    operands = [folded, images] + list(arrays) + ([] if first else list(state))
    vmem = pl.BlockSpec(memory_space=pltpu.VMEM)
    in_specs = [vmem] * len(operands)
    scratch = [
        pltpu.VMEM((texts, DT), jnp.bfloat16),
        pltpu.VMEM((texts, DT), jnp.bfloat16),
        pltpu.VMEM((texts, DS), jnp.bfloat16),
        pltpu.VMEM((texts, DS), jnp.bfloat16),
    ]
    if last:
        operands = [place] + operands
        in_specs = [pl.BlockSpec(memory_space=pltpu.SMEM)] + in_specs
        shapes = [jax.ShapeDtypeStruct((8, ROWS + 8, 128), jnp.float32)]
    else:
        shapes = [
            jax.ShapeDtypeStruct((ROWS, 128), jnp.float32),
            jax.ShapeDtypeStruct((ROWS, DS), jnp.float32),
            jax.ShapeDtypeStruct((ROWS, DS), jnp.float32),
        ]
    flops = 2 * 3 * ROWS * texts * (DT + 3 * DS)

    def body(*refs):
        texts_kernel(len(arrays), first, last, *refs)

    return pl.pallas_call(
        body,
        out_shape=shapes,
        in_specs=in_specs,
        out_specs=[vmem] * len(shapes),
        scratch_shapes=scratch,
        compiler_params=pltpu.CompilerParams(vmem_limit_bytes=VMEM_LIMIT),
        cost_estimate=pl.CostEstimate(
            flops=40 * flops, bytes_accessed=4 * 1024 * 1024, transcendentals=2 * ROWS * texts
        ),
        name="add_texts",
    )(*operands)


def halved(array, index, pairs):
    rows = array.shape[0] // 2
    mine = lax.dynamic_slice_in_dim(array, index * rows, rows, 0)
    other = lax.dynamic_slice_in_dim(array, (1 - index) * rows, rows, 0)
    return mine + move(other, pairs)


def small_call(body, shape, *operands, scalars=0):
    smem, vmem = pl.BlockSpec(memory_space=pltpu.SMEM), pl.BlockSpec(memory_space=pltpu.VMEM)
    return pl.pallas_call(
        body,
        out_shape=jax.ShapeDtypeStruct(shape, jnp.float32),
        in_specs=[smem] * scalars + [vmem] * (len(operands) - scalars),
        out_specs=vmem,
        compiler_params=pltpu.CompilerParams(vmem_limit_bytes=VMEM_LIMIT),
        cost_estimate=pl.CostEstimate(flops=1024, bytes_accessed=1024 * 1024, transcendentals=0),
    )(*operands)


def pack(piece, term, received, scale):
    def body(piece_ref, term_ref, received_ref, out):
        total = scale * (term_ref[...] + received_ref[...])
        for k in range(8):
            out[k, : ROWS // 2] = piece_ref[...]
            for q in range(4):
                here = slice(ROWS // 2 + SHARD * q, ROWS // 2 + SHARD * (q + 1))
                out[k, here] = total[:, 128 * q : 128 * (q + 1)]

    return small_call(body, (8, ROWS, 128), piece, term, received)


def unpack_image(where, pieces, head, scale):
    def body(where_ref, pieces_ref, head_ref, out):
        lane = lax.broadcasted_iota(jnp.int32, (ROWS // 2, 128), 1)
        total = jnp.zeros((ROWS, DS), jnp.float32)
        for half in (0, 1):
            columns = []
            for q in (2 * half, 2 * half + 1):
                a, b = pieces_ref[2 * q, : ROWS // 2], pieces_ref[2 * q + 1, : ROWS // 2]
                top = jnp.where(lane < COLS, a, pltpu.roll(b, COLS, 1))
                bottom = jnp.where(lane < COLS, pltpu.roll(a, COLS, 1), b)
                columns.append(jnp.concatenate([top, bottom], axis=0))
            gap = jnp.concatenate(columns, axis=1)
            start = pl.multiple_of((DS // 2) * lax.rem(where_ref[0] + half, 2), DS // 2)
            total += dot3(split(gap), split(head_ref[pl.ds(start, DS // 2), :]), NN)
        out[...] = scale * total

    return small_call(body, (ROWS, DS), where, pieces, head, scalars=1)


def unpack_head(where, pieces, partner):
    def body(where_ref, pieces_ref, partner_ref, out):
        core = where_ref[1]
        for k in range(8):
            block = lax.rem(k + 4 * where_ref[0], 8) * COLS
            mine = pl.multiple_of(block + core * SHARD, SHARD)
            other = pl.multiple_of(block + (1 - core) * SHARD, SHARD)
            for q in range(4):
                lanes = slice(128 * q, 128 * (q + 1))
                here = slice(ROWS // 2 + SHARD * q, ROWS // 2 + SHARD * (q + 1))
                out[pl.ds(mine, SHARD), lanes] = pieces_ref[k, here]
                out[pl.ds(other, SHARD), lanes] = partner_ref[k, SHARD * q : SHARD * (q + 1)]

    return small_call(body, (DS, DS), where, pieces, partner, scalars=1)


def shards(image_student, image_teacher, text_features, text_teacher, head):
    scale_s = 4.0 / math.sqrt(DS)
    scale_t = 4.0 / math.sqrt(DT)
    batch = ROWS * 32
    xh, core = lax.axis_index("xh"), lax.axis_index("core")
    folded = scale_s * dot(image_student, head, NT)
    images = scale_t * image_teacher

    own = [text_teacher, text_features]
    near = [move(array, CORE) for array in own]
    far = [move(array, X_FLIP) for array in own]
    one = jnp.concatenate([jnp.concatenate(part, axis=1) for part in (own, near)], axis=0)
    *far, _ = lax.optimization_barrier((*far, one))
    last = [move(array, CORE) for array in far]
    two = jnp.concatenate([jnp.concatenate(part, axis=1) for part in (far, last)], axis=0)
    state = add_texts(folded, images, [one, two])
    for step in range(3):
        one, two = move(one, Z_NEXT), move(two, Z_NEXT)
        state = add_texts(folded, images, [one, move(one, CORE)], state)
        state = add_texts(folded, images, [two, move(two, CORE)], state)
    one, two = move(one[:SHARD], Z_NEXT), move(two[:SHARD], Z_NEXT)
    two, *state = lax.optimization_barrier((two, *state))
    state = add_texts(folded, images, [one, move(one, CORE)], state)
    place = jnp.arange(8, dtype=jnp.int32) ^ (4 * xh).astype(jnp.int32)
    (both,) = add_texts(folded, images, [two, move(two, CORE)], state, place)

    got = lax.all_to_all(both, ("xl", "y"), 0, 0, tiled=True)
    stats = got[:, ROWS:].reshape(8, 2, 4, 128)
    stats = stats.transpose(0, 2, 1, 3).reshape(8, 4, ROWS)
    sums = []
    for k in (0, 2):
        tops = stats[:, k]
        top = jnp.max(tops, axis=0)
        shares = jnp.exp(tops - top[None])
        total = jnp.sum(shares * stats[:, k + 1], axis=0)
        shares = shares / total[None]
        lanes = slice(0, COLS) if k == 0 else slice(COLS, 2 * COLS)
        sums.append(jnp.sum(got[:, :ROWS, lanes] * shares[:, :, None], axis=0))
    gap_text = sums[0] - sums[1]

    piece = jnp.concatenate([gap_text[: ROWS // 2], gap_text[ROWS // 2 :]], axis=1)
    term = halved(dot(gap_text, image_student, ((0,), (0,))), core, CORE)
    for pairs in (X_FLIP,) + Z_FOLD[:-1]:
        term = term + move(term, pairs)
    packed = pack(piece, term, move(term, Z_FOLD[-1]), scale_s / math.sqrt(batch))

    pieces = lax.all_to_all(packed, ("xl", "y"), 0, 0, tiled=True)
    partner = move(pieces[:, ROWS // 2 :], CORE)
    where = jnp.stack([xh, core]).astype(jnp.int32)
    return unpack_image(where, pieces, head, scale_s), unpack_head(where, pieces, partner)


def solution(mesh):
    fine = Mesh(mesh.devices.reshape(SIZES), AXES)
    dp, every = ("z", "xh", "core"), AXES
    in_specs = (P(dp, None), P(dp, None), P(every, None), P(every, None), P())
    out_specs = (P(dp, None), P())
    return jax.shard_map(shards, mesh=fine, in_specs=in_specs, out_specs=out_specs, check_vma=False)
```

```python
import math

import jax
import jax.numpy as jnp
from jax import lax
from jax.experimental import pallas as pl
from jax.experimental.pallas import tpu as pltpu
from jax.sharding import Mesh, PartitionSpec as P

AXES = ("z", "xh", "core", "xl", "y")
SIZES = (8, 2, 2, 2, 4)
HIGH = lax.Precision.HIGH
DS, DT = 512, 768
ROWS = 256
SHARD = 32
COLS = DS // 8
VMEM_LIMIT = 14 * 1024 * 1024


def linear(z, xh, core, xl, y):
    return (((z * 2 + xh) * 2 + core) * 2 + xl) * 4 + y


def moves(place):
    pairs = []
    for z in range(8):
        for xh in range(2):
            for core in range(2):
                for xl in range(2):
                    for y in range(4):
                        here = (z, xh, core, xl, y)
                        pairs.append((linear(*here), linear(*place(*here))))
    return pairs


Z_NEXT = moves(lambda z, xh, core, xl, y: ((z + 1 - 2 * core) % 8, xh, core, xl, y))
X_FLIP = moves(lambda z, xh, core, xl, y: (z, 1 - xh, core, 1 - xl, y))
CORE = moves(lambda z, xh, core, xl, y: (z, xh, 1 - core, xl, y))
Z_FOLD = tuple(
    moves(lambda z, xh, core, xl, y, bit=bit: (z ^ bit, xh, core, xl, y)) for bit in (1, 2, 6)
)


def move(array, pairs):
    return lax.ppermute(array, AXES, pairs)


def dot(a, b, dims):
    return lax.dot_general(
        a, b, (dims, ((), ())), precision=HIGH, preferred_element_type=jnp.float32
    )


def split(x):
    high = x.astype(jnp.bfloat16)
    return high, (x - high.astype(jnp.float32)).astype(jnp.bfloat16)


def dot3(a, b, dims):
    def one(p, q):
        return lax.dot_general(p, q, (dims, ((), ())), preferred_element_type=jnp.float32)

    return one(a[0], b[0]) + (one(a[0], b[1]) + one(a[1], b[0]))


NT = ((1,), (1,))
NN = ((1,), (0,))


def texts_kernel(count, first, last, *refs):
    refs = list(refs)
    place = refs.pop(0) if last else None
    folded_ref, images_ref = refs.pop(0), refs.pop(0)
    arrays = [refs.pop(0) for _ in range(count)]
    state = None if first else [refs.pop(0) for _ in range(3)]
    outs = [refs.pop(0) for _ in range(1 if last else 3)]
    t_high, t_low, f_high, f_low = refs
    start = 0
    for array in arrays:
        here = pl.ds(start, array.shape[0])
        start += array.shape[0]
        t_high[here, :], t_low[here, :] = split(array[:, :DT])
        f_high[here, :], f_low[here, :] = split(array[:, DT:])
    texts = (t_high[...], t_low[...])
    features = (f_high[...], f_low[...])
    tiles = (
        dot3(split(folded_ref[...]), features, NT),
        dot3(split(images_ref[...]), texts, NT),
    )
    lane = lax.broadcasted_iota(jnp.int32, (ROWS, 128), 1)
    stats = jnp.zeros((ROWS, 128), jnp.float32)
    products = []
    for k, tile in enumerate(tiles):
        top = jnp.max(tile, axis=1, keepdims=True)
        if not first:
            old_top = state[0][:, 2 * k : 2 * k + 1]
            top = jnp.maximum(top, old_top)
        weight = jnp.exp(tile - top)
        total = jnp.sum(weight, axis=1, keepdims=True)
        product = dot3(split(weight), features, NN)
        if not first:
            shrink = jnp.exp(old_top - top)
            total = total + shrink * state[0][:, 2 * k + 1 : 2 * k + 2]
            product = product + shrink * state[1 + k][...]
        stats = jnp.where(lane == 2 * k, top, stats)
        stats = jnp.where(lane == 2 * k + 1, total, stats)
        products.append(product)
    if not last:
        outs[0][...] = stats
        outs[1][...] = products[0]
        outs[2][...] = products[1]
        return
    out = outs[0]
    turned = stats.T[:8]
    for q in range(4):
        a = products[0][:, 128 * q : 128 * q + 128]
        b = products[1][:, 128 * q : 128 * q + 128]
        out[place[2 * q], 0:ROWS] = jnp.where(lane < COLS, a, pltpu.roll(b, COLS, 1))
        out[place[2 * q + 1], 0:ROWS] = jnp.where(lane < COLS, pltpu.roll(a, COLS, 1), b)
    for k in range(8):
        out[k, ROWS : ROWS + 4] = turned[:4, :128]
        out[k, ROWS + 4 : ROWS + 8] = turned[:4, 128:]


def add_texts(folded, images, arrays, state=None, place=None):
    first, last = state is None, place is not None
    texts = sum(array.shape[0] for array in arrays)
    operands = [folded, images] + list(arrays) + ([] if first else list(state))
    vmem = pl.BlockSpec(memory_space=pltpu.VMEM)
    in_specs = [vmem] * len(operands)
    scratch = [
        pltpu.VMEM((texts, DT), jnp.bfloat16),
        pltpu.VMEM((texts, DT), jnp.bfloat16),
        pltpu.VMEM((texts, DS), jnp.bfloat16),
        pltpu.VMEM((texts, DS), jnp.bfloat16),
    ]
    if last:
        operands = [place] + operands
        in_specs = [pl.BlockSpec(memory_space=pltpu.SMEM)] + in_specs
        shapes = [jax.ShapeDtypeStruct((8, ROWS + 8, 128), jnp.float32)]
    else:
        shapes = [
            jax.ShapeDtypeStruct((ROWS, 128), jnp.float32),
            jax.ShapeDtypeStruct((ROWS, DS), jnp.float32),
            jax.ShapeDtypeStruct((ROWS, DS), jnp.float32),
        ]
    flops = 2 * 3 * ROWS * texts * (DT + 3 * DS)

    def body(*refs):
        texts_kernel(len(arrays), first, last, *refs)

    return pl.pallas_call(
        body,
        out_shape=shapes,
        in_specs=in_specs,
        out_specs=[vmem] * len(shapes),
        scratch_shapes=scratch,
        compiler_params=pltpu.CompilerParams(vmem_limit_bytes=VMEM_LIMIT),
        cost_estimate=pl.CostEstimate(
            flops=40 * flops, bytes_accessed=4 * 1024 * 1024, transcendentals=2 * ROWS * texts
        ),
        name="add_texts",
    )(*operands)


def halved(array, starts, pairs):
    shape = (array.shape[0] // 2, array.shape[1])
    mine, other = [lax.dynamic_slice(array, (at, jnp.uint32(0)), shape) for at in starts]
    return mine + move(other, pairs)


def small_call(body, shape, *operands, scalars=0):
    smem, vmem = pl.BlockSpec(memory_space=pltpu.SMEM), pl.BlockSpec(memory_space=pltpu.VMEM)
    return pl.pallas_call(
        body,
        out_shape=jax.ShapeDtypeStruct(shape, jnp.float32),
        in_specs=[smem] * scalars + [vmem] * (len(operands) - scalars),
        out_specs=vmem,
        compiler_params=pltpu.CompilerParams(vmem_limit_bytes=VMEM_LIMIT),
        cost_estimate=pl.CostEstimate(flops=1024, bytes_accessed=1024 * 1024, transcendentals=0),
    )(*operands)


def pack(piece, term, received, scale):
    def body(piece_ref, term_ref, received_ref, out):
        total = scale * (term_ref[...] + received_ref[...])
        for k in range(8):
            out[k, : ROWS // 2] = piece_ref[...]
            for q in range(4):
                here = slice(ROWS // 2 + SHARD * q, ROWS // 2 + SHARD * (q + 1))
                out[k, here] = total[:, 128 * q : 128 * (q + 1)]

    return small_call(body, (8, ROWS, 128), piece, term, received)


def unpack_image(where, pieces, head, scale):
    def body(where_ref, pieces_ref, head_ref, out):
        lane = lax.broadcasted_iota(jnp.int32, (ROWS // 2, 128), 1)
        total = jnp.zeros((ROWS, DS), jnp.float32)
        for half in (0, 1):
            columns = []
            for q in (2 * half, 2 * half + 1):
                a, b = pieces_ref[2 * q, : ROWS // 2], pieces_ref[2 * q + 1, : ROWS // 2]
                top = jnp.where(lane < COLS, a, pltpu.roll(b, COLS, 1))
                bottom = jnp.where(lane < COLS, pltpu.roll(a, COLS, 1), b)
                columns.append(jnp.concatenate([top, bottom], axis=0))
            gap = jnp.concatenate(columns, axis=1)
            start = pl.multiple_of((DS // 2) * lax.rem(where_ref[0] + half, 2), DS // 2)
            total += dot3(split(gap), split(head_ref[pl.ds(start, DS // 2), :]), NN)
        out[...] = scale * total

    return small_call(body, (ROWS, DS), where, pieces, head, scalars=1)


def unpack_head(where, pieces, partner):
    def body(where_ref, pieces_ref, partner_ref, out):
        core = where_ref[1]
        for k in range(8):
            block = lax.rem(k + 4 * where_ref[0], 8) * COLS
            mine = pl.multiple_of(block + core * SHARD, SHARD)
            other = pl.multiple_of(block + (1 - core) * SHARD, SHARD)
            for q in range(4):
                lanes = slice(128 * q, 128 * (q + 1))
                here = slice(ROWS // 2 + SHARD * q, ROWS // 2 + SHARD * (q + 1))
                out[pl.ds(mine, SHARD), lanes] = pieces_ref[k, here]
                out[pl.ds(other, SHARD), lanes] = partner_ref[k, SHARD * q : SHARD * (q + 1)]

    return small_call(body, (DS, DS), where, pieces, partner, scalars=1)


def shards(image_student, image_teacher, text_features, text_teacher, head):
    scale_s = 4.0 / math.sqrt(DS)
    scale_t = 4.0 / math.sqrt(DT)
    batch = ROWS * 32
    xh, core = lax.axis_index("xh"), lax.axis_index("core")
    folded = scale_s * dot(image_student, head, NT)
    images = scale_t * image_teacher

    own = [text_teacher, text_features]
    near = [move(array, CORE) for array in own]
    far = [move(array, X_FLIP) for array in own]
    one = jnp.concatenate([jnp.concatenate(part, axis=1) for part in (own, near)], axis=0)
    *far, _ = lax.optimization_barrier((*far, one))
    last = [move(array, CORE) for array in far]
    two = jnp.concatenate([jnp.concatenate(part, axis=1) for part in (far, last)], axis=0)
    state = add_texts(folded, images, [one, two])
    for step in range(3):
        one, two = move(one, Z_NEXT), move(two, Z_NEXT)
        state = add_texts(folded, images, [one, move(one, CORE)], state)
        state = add_texts(folded, images, [two, move(two, CORE)], state)
    one, two = move(one[:SHARD], Z_NEXT), move(two[:SHARD], Z_NEXT)
    two, *state = lax.optimization_barrier((two, *state))
    state = add_texts(folded, images, [one, move(one, CORE)], state)
    place = jnp.arange(8, dtype=jnp.int32) ^ (4 * xh).astype(jnp.int32)
    (both,) = add_texts(folded, images, [two, move(two, CORE)], state, place)

    starts = [(core * SHARD).astype(jnp.uint32), ((1 - core) * SHARD).astype(jnp.uint32)]
    both, *starts = lax.optimization_barrier((both, *starts))
    got = lax.all_to_all(both, ("xl", "y"), 0, 0, tiled=True)
    stats = got[:, ROWS:].reshape(8, 2, 4, 128)
    stats = stats.transpose(0, 2, 1, 3).reshape(8, 4, ROWS)
    sums = []
    for k in (0, 2):
        tops = stats[:, k]
        top = jnp.max(tops, axis=0)
        shares = jnp.exp(tops - top[None])
        total = jnp.sum(shares * stats[:, k + 1], axis=0)
        shares = shares / total[None]
        lanes = slice(0, COLS) if k == 0 else slice(COLS, 2 * COLS)
        sums.append(jnp.sum(got[:, :ROWS, lanes] * shares[:, :, None], axis=0))
    gap_text = sums[0] - sums[1]

    piece = jnp.concatenate([gap_text[: ROWS // 2], gap_text[ROWS // 2 :]], axis=1)
    term = halved(dot(gap_text, image_student, ((0,), (0,))), starts, CORE)
    for pairs in (X_FLIP,) + Z_FOLD[:-1]:
        term = term + move(term, pairs)
    packed = pack(piece, term, move(term, Z_FOLD[-1]), scale_s / math.sqrt(batch))

    pieces = lax.all_to_all(packed, ("xl", "y"), 0, 0, tiled=True)
    partner = move(pieces[:, ROWS // 2 :], CORE)
    where = jnp.stack([xh, core]).astype(jnp.int32)
    return unpack_image(where, pieces, head, scale_s), unpack_head(where, pieces, partner)


def solution(mesh):
    fine = Mesh(mesh.devices.reshape(SIZES), AXES)
    dp, every = ("z", "xh", "core"), AXES
    in_specs = (P(dp, None), P(dp, None), P(every, None), P(every, None), P())
    out_specs = (P(dp, None), P())
    return jax.shard_map(shards, mesh=fine, in_specs=in_specs, out_specs=out_specs, check_vma=False)
```

```python
import math

import jax
import jax.numpy as jnp
from jax import lax
from jax.experimental import pallas as pl
from jax.experimental.pallas import tpu as pltpu
from jax.sharding import Mesh, PartitionSpec as P

AXES = ("z", "xh", "core", "xl", "y")
SIZES = (8, 2, 2, 2, 4)
HIGH = lax.Precision.HIGH
DS, DT = 512, 768
ROWS = 256
SHARD = 32
COLS = DS // 8
VMEM_LIMIT = 14 * 1024 * 1024


def linear(z, xh, core, xl, y):
    return (((z * 2 + xh) * 2 + core) * 2 + xl) * 4 + y


def moves(place):
    pairs = []
    for z in range(8):
        for xh in range(2):
            for core in range(2):
                for xl in range(2):
                    for y in range(4):
                        here = (z, xh, core, xl, y)
                        pairs.append((linear(*here), linear(*place(*here))))
    return pairs


Z_NEXT = moves(lambda z, xh, core, xl, y: ((z + 1 - 2 * core) % 8, xh, core, xl, y))
X_FLIP = moves(lambda z, xh, core, xl, y: (z, 1 - xh, core, 1 - xl, y))
CORE = moves(lambda z, xh, core, xl, y: (z, xh, 1 - core, xl, y))
Z_FOLD = tuple(
    moves(lambda z, xh, core, xl, y, bit=bit: (z ^ bit, xh, core, xl, y)) for bit in (1, 2, 6)
)


def move(array, pairs):
    return lax.ppermute(array, AXES, pairs)


def dot(a, b, dims):
    return lax.dot_general(
        a, b, (dims, ((), ())), precision=HIGH, preferred_element_type=jnp.float32
    )


def split(x):
    high = x.astype(jnp.bfloat16)
    return high, (x - high.astype(jnp.float32)).astype(jnp.bfloat16)


def dot3(a, b, dims):
    def one(p, q):
        return lax.dot_general(p, q, (dims, ((), ())), preferred_element_type=jnp.float32)

    return one(a[0], b[0]) + (one(a[0], b[1]) + one(a[1], b[0]))


NT = ((1,), (1,))
NN = ((1,), (0,))


def texts_kernel(count, first, last, *refs):
    refs = list(refs)
    place = refs.pop(0) if last else None
    folded_ref, images_ref = refs.pop(0), refs.pop(0)
    arrays = [refs.pop(0) for _ in range(count)]
    state = None if first else [refs.pop(0) for _ in range(3)]
    outs = [refs.pop(0) for _ in range(1 if last else 3)]
    t_high, t_low, f_high, f_low = refs
    start = 0
    for array in arrays:
        here = pl.ds(start, array.shape[0])
        start += array.shape[0]
        t_high[here, :], t_low[here, :] = split(array[:, :DT])
        f_high[here, :], f_low[here, :] = split(array[:, DT:])
    texts = (t_high[...], t_low[...])
    features = (f_high[...], f_low[...])
    tiles = (
        dot3(split(folded_ref[...]), features, NT),
        dot3(split(images_ref[...]), texts, NT),
    )
    lane = lax.broadcasted_iota(jnp.int32, (ROWS, 128), 1)
    stats = jnp.zeros((ROWS, 128), jnp.float32)
    products = []
    for k, tile in enumerate(tiles):
        top = jnp.max(tile, axis=1, keepdims=True)
        if not first:
            old_top = state[0][:, 2 * k : 2 * k + 1]
            top = jnp.maximum(top, old_top)
        weight = jnp.exp(tile - top)
        total = jnp.sum(weight, axis=1, keepdims=True)
        product = dot3(split(weight), features, NN)
        if not first:
            shrink = jnp.exp(old_top - top)
            total = total + shrink * state[0][:, 2 * k + 1 : 2 * k + 2]
            product = product + shrink * state[1 + k][...]
        stats = jnp.where(lane == 2 * k, top, stats)
        stats = jnp.where(lane == 2 * k + 1, total, stats)
        products.append(product)
    if not last:
        outs[0][...] = stats
        outs[1][...] = products[0]
        outs[2][...] = products[1]
        return
    out = outs[0]
    turned = stats.T[:8]
    for q in range(4):
        a = products[0][:, 128 * q : 128 * q + 128]
        b = products[1][:, 128 * q : 128 * q + 128]
        out[place[2 * q], 0:ROWS] = jnp.where(lane < COLS, a, pltpu.roll(b, COLS, 1))
        out[place[2 * q + 1], 0:ROWS] = jnp.where(lane < COLS, pltpu.roll(a, COLS, 1), b)
    for k in range(8):
        out[k, ROWS : ROWS + 4] = turned[:4, :128]
        out[k, ROWS + 4 : ROWS + 8] = turned[:4, 128:]


def add_texts(folded, images, arrays, state=None, place=None):
    first, last = state is None, place is not None
    texts = sum(array.shape[0] for array in arrays)
    operands = [folded, images] + list(arrays) + ([] if first else list(state))
    vmem = pl.BlockSpec(memory_space=pltpu.VMEM)
    in_specs = [vmem] * len(operands)
    scratch = [
        pltpu.VMEM((texts, DT), jnp.bfloat16),
        pltpu.VMEM((texts, DT), jnp.bfloat16),
        pltpu.VMEM((texts, DS), jnp.bfloat16),
        pltpu.VMEM((texts, DS), jnp.bfloat16),
    ]
    if last:
        operands = [place] + operands
        in_specs = [pl.BlockSpec(memory_space=pltpu.SMEM)] + in_specs
        shapes = [jax.ShapeDtypeStruct((8, ROWS + 8, 128), jnp.float32)]
    else:
        shapes = [
            jax.ShapeDtypeStruct((ROWS, 128), jnp.float32),
            jax.ShapeDtypeStruct((ROWS, DS), jnp.float32),
            jax.ShapeDtypeStruct((ROWS, DS), jnp.float32),
        ]
    flops = 2 * 3 * ROWS * texts * (DT + 3 * DS)

    def body(*refs):
        texts_kernel(len(arrays), first, last, *refs)

    return pl.pallas_call(
        body,
        out_shape=shapes,
        in_specs=in_specs,
        out_specs=[vmem] * len(shapes),
        scratch_shapes=scratch,
        compiler_params=pltpu.CompilerParams(vmem_limit_bytes=VMEM_LIMIT),
        cost_estimate=pl.CostEstimate(
            flops=40 * flops, bytes_accessed=4 * 1024 * 1024, transcendentals=2 * ROWS * texts
        ),
        name="add_texts",
    )(*operands)


def halved(array, starts, pairs):
    shape = (array.shape[0] // 2, array.shape[1])
    mine, other = [lax.dynamic_slice(array, (at, jnp.uint32(0)), shape) for at in starts]
    return mine + move(other, pairs)


def small_call(body, shape, *operands, scalars=0):
    smem, vmem = pl.BlockSpec(memory_space=pltpu.SMEM), pl.BlockSpec(memory_space=pltpu.VMEM)
    return pl.pallas_call(
        body,
        out_shape=jax.ShapeDtypeStruct(shape, jnp.float32),
        in_specs=[smem] * scalars + [vmem] * (len(operands) - scalars),
        out_specs=vmem,
        compiler_params=pltpu.CompilerParams(vmem_limit_bytes=VMEM_LIMIT),
        cost_estimate=pl.CostEstimate(flops=1024, bytes_accessed=1024 * 1024, transcendentals=0),
    )(*operands)


def pack(piece, term, received, scale):
    def body(piece_ref, term_ref, received_ref, out):
        total = scale * (term_ref[...] + received_ref[...])
        for k in range(8):
            out[k, : ROWS // 2] = piece_ref[...]
            for q in range(4):
                here = slice(ROWS // 2 + SHARD * q, ROWS // 2 + SHARD * (q + 1))
                out[k, here] = total[:, 128 * q : 128 * (q + 1)]

    return small_call(body, (8, ROWS, 128), piece, term, received)


def unpack_image(where, pieces, head, scale):
    def body(where_ref, pieces_ref, head_ref, out):
        lane = lax.broadcasted_iota(jnp.int32, (ROWS // 2, 128), 1)
        total = jnp.zeros((ROWS, DS), jnp.float32)
        for half in (0, 1):
            columns = []
            for q in (2 * half, 2 * half + 1):
                a, b = pieces_ref[2 * q, : ROWS // 2], pieces_ref[2 * q + 1, : ROWS // 2]
                top = jnp.where(lane < COLS, a, pltpu.roll(b, COLS, 1))
                bottom = jnp.where(lane < COLS, pltpu.roll(a, COLS, 1), b)
                columns.append(jnp.concatenate([top, bottom], axis=0))
            gap = jnp.concatenate(columns, axis=1)
            start = pl.multiple_of((DS // 2) * lax.rem(where_ref[0] + half, 2), DS // 2)
            total += dot3(split(gap), split(head_ref[pl.ds(start, DS // 2), :]), NN)
        out[...] = scale * total

    return small_call(body, (ROWS, DS), where, pieces, head, scalars=1)


def unpack_head(where, pieces, partner):
    def body(where_ref, pieces_ref, partner_ref, out):
        core = where_ref[1]
        for k in range(8):
            block = lax.rem(k + 4 * where_ref[0], 8) * COLS
            mine = pl.multiple_of(block + core * SHARD, SHARD)
            other = pl.multiple_of(block + (1 - core) * SHARD, SHARD)
            for q in range(4):
                lanes = slice(128 * q, 128 * (q + 1))
                here = slice(ROWS // 2 + SHARD * q, ROWS // 2 + SHARD * (q + 1))
                out[pl.ds(mine, SHARD), lanes] = pieces_ref[k, here]
                out[pl.ds(other, SHARD), lanes] = partner_ref[k, SHARD * q : SHARD * (q + 1)]

    return small_call(body, (DS, DS), where, pieces, partner, scalars=1)


def shards(image_student, image_teacher, text_features, text_teacher, head):
    scale_s = 4.0 / math.sqrt(DS)
    scale_t = 4.0 / math.sqrt(DT)
    batch = ROWS * 32
    xh, core = lax.axis_index("xh"), lax.axis_index("core")

    own = [text_teacher, text_features]
    near = [move(array, CORE) for array in own]
    far = [move(array, X_FLIP) for array in own]
    one = jnp.concatenate([jnp.concatenate(part, axis=1) for part in (own, near)], axis=0)
    *far, _ = lax.optimization_barrier((*far, one))
    last = [move(array, CORE) for array in far]
    two = jnp.concatenate([jnp.concatenate(part, axis=1) for part in (far, last)], axis=0)
    students, _ = lax.optimization_barrier((image_student, one))
    folded = scale_s * dot(students, head, NT)
    images = scale_t * image_teacher
    state = add_texts(folded, images, [one, two])
    for step in range(3):
        one, two = move(one, Z_NEXT), move(two, Z_NEXT)
        state = add_texts(folded, images, [one, move(one, CORE)], state)
        if step == 2:
            one = move(one[:SHARD], Z_NEXT)
            one, *state = lax.optimization_barrier((one, *state))
        state = add_texts(folded, images, [two, move(two, CORE)], state)
    two = move(two[:SHARD], Z_NEXT)
    two, *state = lax.optimization_barrier((two, *state))
    state = add_texts(folded, images, [one, move(one, CORE)], state)
    place = jnp.arange(8, dtype=jnp.int32) ^ (4 * xh).astype(jnp.int32)
    (both,) = add_texts(folded, images, [two, move(two, CORE)], state, place)

    starts = [(core * SHARD).astype(jnp.uint32), ((1 - core) * SHARD).astype(jnp.uint32)]
    both, *starts = lax.optimization_barrier((both, *starts))
    got = lax.all_to_all(both, ("xl", "y"), 0, 0, tiled=True)
    stats = got[:, ROWS:].reshape(8, 2, 4, 128)
    stats = stats.transpose(0, 2, 1, 3).reshape(8, 4, ROWS)
    sums = []
    for k in (0, 2):
        tops = stats[:, k]
        top = jnp.max(tops, axis=0)
        shares = jnp.exp(tops - top[None])
        total = jnp.sum(shares * stats[:, k + 1], axis=0)
        shares = shares / total[None]
        lanes = slice(0, COLS) if k == 0 else slice(COLS, 2 * COLS)
        sums.append(jnp.sum(got[:, :ROWS, lanes] * shares[:, :, None], axis=0))
    gap_text = sums[0] - sums[1]

    piece = jnp.concatenate([gap_text[: ROWS // 2], gap_text[ROWS // 2 :]], axis=1)
    term = halved(dot(gap_text, image_student, ((0,), (0,))), starts, CORE)
    for pairs in (X_FLIP,) + Z_FOLD[:-1]:
        term = term + move(term, pairs)
    packed = pack(piece, term, move(term, Z_FOLD[-1]), scale_s / math.sqrt(batch))

    pieces = lax.all_to_all(packed, ("xl", "y"), 0, 0, tiled=True)
    partner = move(pieces[:, ROWS // 2 :], CORE)
    where = jnp.stack([xh, core]).astype(jnp.int32)
    return unpack_image(where, pieces, head, scale_s), unpack_head(where, pieces, partner)


def solution(mesh):
    fine = Mesh(mesh.devices.reshape(SIZES), AXES)
    dp, every = ("z", "xh", "core"), AXES
    in_specs = (P(dp, None), P(dp, None), P(every, None), P(every, None), P())
    out_specs = (P(dp, None), P())
    return jax.shard_map(shards, mesh=fine, in_specs=in_specs, out_specs=out_specs, check_vma=False)
```

```python
import math

import jax
import jax.numpy as jnp
from jax import lax
from jax.experimental import pallas as pl
from jax.experimental.pallas import tpu as pltpu
from jax.sharding import Mesh, PartitionSpec as P

AXES = ("z", "xh", "core", "xl", "y")
SIZES = (8, 2, 2, 2, 4)
HIGH = lax.Precision.HIGH
DS, DT = 512, 768
ROWS = 256
SHARD = 32
COLS = DS // 8
VMEM_LIMIT = 14 * 1024 * 1024


def linear(z, xh, core, xl, y):
    return (((z * 2 + xh) * 2 + core) * 2 + xl) * 4 + y


def moves(place):
    pairs = []
    for z in range(8):
        for xh in range(2):
            for core in range(2):
                for xl in range(2):
                    for y in range(4):
                        here = (z, xh, core, xl, y)
                        pairs.append((linear(*here), linear(*place(*here))))
    return pairs


Z_NEXT = moves(lambda z, xh, core, xl, y: ((z + 1 - 2 * core) % 8, xh, core, xl, y))
X_FLIP = moves(lambda z, xh, core, xl, y: (z, 1 - xh, core, 1 - xl, y))
CORE = moves(lambda z, xh, core, xl, y: (z, xh, 1 - core, xl, y))
Z_FOLD = tuple(
    moves(lambda z, xh, core, xl, y, bit=bit: (z ^ bit, xh, core, xl, y)) for bit in (1, 2, 6)
)


def move(array, pairs):
    return lax.ppermute(array, AXES, pairs)


def dot(a, b, dims):
    return lax.dot_general(
        a, b, (dims, ((), ())), precision=HIGH, preferred_element_type=jnp.float32
    )


def split(x):
    high = x.astype(jnp.bfloat16)
    return high, (x - high.astype(jnp.float32)).astype(jnp.bfloat16)


def dot3(a, b, dims):
    def one(p, q):
        return lax.dot_general(p, q, (dims, ((), ())), preferred_element_type=jnp.float32)

    return one(a[0], b[0]) + (one(a[0], b[1]) + one(a[1], b[0]))


NT = ((1,), (1,))
NN = ((1,), (0,))


def texts_kernel(count, first, last, *refs):
    refs = list(refs)
    place = refs.pop(0) if last else None
    folded_ref, images_ref = refs.pop(0), refs.pop(0)
    arrays = [refs.pop(0) for _ in range(count)]
    state = None if first else [refs.pop(0) for _ in range(3)]
    outs = [refs.pop(0) for _ in range(1 if last else 3)]
    t_high, t_low, f_high, f_low = refs
    start = 0
    for array in arrays:
        here = pl.ds(start, array.shape[0])
        start += array.shape[0]
        t_high[here, :], t_low[here, :] = split(array[:, :DT])
        f_high[here, :], f_low[here, :] = split(array[:, DT:])
    texts = (t_high[...], t_low[...])
    features = (f_high[...], f_low[...])
    tiles = (
        dot3(split(folded_ref[...]), features, NT),
        dot3(split(images_ref[...]), texts, NT),
    )
    lane = lax.broadcasted_iota(jnp.int32, (ROWS, 128), 1)
    stats = jnp.zeros((ROWS, 128), jnp.float32)
    products = []
    for k, tile in enumerate(tiles):
        top = jnp.max(tile, axis=1, keepdims=True)
        if not first:
            old_top = state[0][:, 2 * k : 2 * k + 1]
            top = jnp.maximum(top, old_top)
        weight = jnp.exp(tile - top)
        total = jnp.sum(weight, axis=1, keepdims=True)
        product = dot3(split(weight), features, NN)
        if not first:
            shrink = jnp.exp(old_top - top)
            total = total + shrink * state[0][:, 2 * k + 1 : 2 * k + 2]
            product = product + shrink * state[1 + k][...]
        stats = jnp.where(lane == 2 * k, top, stats)
        stats = jnp.where(lane == 2 * k + 1, total, stats)
        products.append(product)
    if not last:
        outs[0][...] = stats
        outs[1][...] = products[0]
        outs[2][...] = products[1]
        return
    out = outs[0]
    turned = stats.T[:8]
    for q in range(4):
        a = products[0][:, 128 * q : 128 * q + 128]
        b = products[1][:, 128 * q : 128 * q + 128]
        out[place[2 * q], 0:ROWS] = jnp.where(lane < COLS, a, pltpu.roll(b, COLS, 1))
        out[place[2 * q + 1], 0:ROWS] = jnp.where(lane < COLS, pltpu.roll(a, COLS, 1), b)
    for k in range(8):
        out[k, ROWS : ROWS + 4] = turned[:4, :128]
        out[k, ROWS + 4 : ROWS + 8] = turned[:4, 128:]


def add_texts(folded, images, arrays, state=None, place=None):
    first, last = state is None, place is not None
    texts = sum(array.shape[0] for array in arrays)
    operands = [folded, images] + list(arrays) + ([] if first else list(state))
    vmem = pl.BlockSpec(memory_space=pltpu.VMEM)
    in_specs = [vmem] * len(operands)
    scratch = [
        pltpu.VMEM((texts, DT), jnp.bfloat16),
        pltpu.VMEM((texts, DT), jnp.bfloat16),
        pltpu.VMEM((texts, DS), jnp.bfloat16),
        pltpu.VMEM((texts, DS), jnp.bfloat16),
    ]
    if last:
        operands = [place] + operands
        in_specs = [pl.BlockSpec(memory_space=pltpu.SMEM)] + in_specs
        shapes = [jax.ShapeDtypeStruct((8, ROWS + 8, 128), jnp.float32)]
    else:
        shapes = [
            jax.ShapeDtypeStruct((ROWS, 128), jnp.float32),
            jax.ShapeDtypeStruct((ROWS, DS), jnp.float32),
            jax.ShapeDtypeStruct((ROWS, DS), jnp.float32),
        ]
    flops = 2 * 3 * ROWS * texts * (DT + 3 * DS)

    def body(*refs):
        texts_kernel(len(arrays), first, last, *refs)

    return pl.pallas_call(
        body,
        out_shape=shapes,
        in_specs=in_specs,
        out_specs=[vmem] * len(shapes),
        scratch_shapes=scratch,
        compiler_params=pltpu.CompilerParams(vmem_limit_bytes=VMEM_LIMIT),
        cost_estimate=pl.CostEstimate(
            flops=40 * flops, bytes_accessed=4 * 1024 * 1024, transcendentals=2 * ROWS * texts
        ),
        name="add_texts",
    )(*operands)


def halved(array, starts, pairs):
    shape = (array.shape[0] // 2, array.shape[1])
    mine, other = [lax.dynamic_slice(array, (at, jnp.uint32(0)), shape) for at in starts]
    return mine + move(other, pairs)


def small_call(body, shape, *operands, scalars=0):
    smem, vmem = pl.BlockSpec(memory_space=pltpu.SMEM), pl.BlockSpec(memory_space=pltpu.VMEM)
    return pl.pallas_call(
        body,
        out_shape=jax.ShapeDtypeStruct(shape, jnp.float32),
        in_specs=[smem] * scalars + [vmem] * (len(operands) - scalars),
        out_specs=vmem,
        compiler_params=pltpu.CompilerParams(vmem_limit_bytes=VMEM_LIMIT),
        cost_estimate=pl.CostEstimate(flops=1024, bytes_accessed=1024 * 1024, transcendentals=0),
    )(*operands)


def pack(piece, term, received, scale):
    def body(piece_ref, term_ref, received_ref, out):
        total = scale * (term_ref[...] + received_ref[...])
        for k in range(8):
            out[k, : ROWS // 2] = piece_ref[...]
            for q in range(4):
                here = slice(ROWS // 2 + SHARD * q, ROWS // 2 + SHARD * (q + 1))
                out[k, here] = total[:, 128 * q : 128 * (q + 1)]

    return small_call(body, (8, ROWS, 128), piece, term, received)


def unpack_image(where, pieces, head, scale):
    def body(where_ref, pieces_ref, head_ref, out):
        lane = lax.broadcasted_iota(jnp.int32, (ROWS // 2, 128), 1)
        total = jnp.zeros((ROWS, DS), jnp.float32)
        for half in (0, 1):
            columns = []
            for q in (2 * half, 2 * half + 1):
                a, b = pieces_ref[2 * q, : ROWS // 2], pieces_ref[2 * q + 1, : ROWS // 2]
                top = jnp.where(lane < COLS, a, pltpu.roll(b, COLS, 1))
                bottom = jnp.where(lane < COLS, pltpu.roll(a, COLS, 1), b)
                columns.append(jnp.concatenate([top, bottom], axis=0))
            gap = jnp.concatenate(columns, axis=1)
            start = pl.multiple_of((DS // 2) * lax.rem(where_ref[0] + half, 2), DS // 2)
            total += dot3(split(gap), split(head_ref[pl.ds(start, DS // 2), :]), NN)
        out[...] = scale * total

    return small_call(body, (ROWS, DS), where, pieces, head, scalars=1)


def unpack_head(where, pieces, partner):
    def body(where_ref, pieces_ref, partner_ref, out):
        core = where_ref[1]
        for k in range(8):
            block = lax.rem(k + 4 * where_ref[0], 8) * COLS
            mine = pl.multiple_of(block + core * SHARD, SHARD)
            other = pl.multiple_of(block + (1 - core) * SHARD, SHARD)
            for q in range(4):
                lanes = slice(128 * q, 128 * (q + 1))
                here = slice(ROWS // 2 + SHARD * q, ROWS // 2 + SHARD * (q + 1))
                out[pl.ds(mine, SHARD), lanes] = pieces_ref[k, here]
                out[pl.ds(other, SHARD), lanes] = partner_ref[k, SHARD * q : SHARD * (q + 1)]

    return small_call(body, (DS, DS), where, pieces, partner, scalars=1)


def shards(image_student, image_teacher, text_features, text_teacher, head):
    scale_s = 4.0 / math.sqrt(DS)
    scale_t = 4.0 / math.sqrt(DT)
    batch = ROWS * 32
    xh, core = lax.axis_index("xh"), lax.axis_index("core")

    own = [text_teacher, text_features]
    near = [move(array, CORE) for array in own]
    far = [move(array, X_FLIP) for array in own]
    one = jnp.concatenate([jnp.concatenate(part, axis=1) for part in (own, near)], axis=0)
    *far, _ = lax.optimization_barrier((*far, one))
    last = [move(array, CORE) for array in far]
    two = jnp.concatenate([jnp.concatenate(part, axis=1) for part in (far, last)], axis=0)
    students, _ = lax.optimization_barrier((image_student, one))
    folded = scale_s * dot(students, head, NT)
    images = scale_t * image_teacher
    state = add_texts(folded, images, [one, two])
    for step in range(3):
        one, two = move(one, Z_NEXT), move(two, Z_NEXT)
        state = add_texts(folded, images, [one, move(one, CORE)], state)
        if step == 2:
            one = move(one[:SHARD], Z_NEXT)
            one, *state = lax.optimization_barrier((one, *state))
        state = add_texts(folded, images, [two, move(two, CORE)], state)
    two = move(two[:SHARD], Z_NEXT)
    two, *state = lax.optimization_barrier((two, *state))
    state = add_texts(folded, images, [one, move(one, CORE)], state)
    place = jnp.arange(8, dtype=jnp.int32) ^ (4 * xh).astype(jnp.int32)
    (both,) = add_texts(folded, images, [two, move(two, CORE)], state, place)

    starts = [(core * SHARD).astype(jnp.uint32), ((1 - core) * SHARD).astype(jnp.uint32)]
    both, *starts = lax.optimization_barrier((both, *starts))
    got = lax.all_to_all(both, ("xl", "y"), 0, 0, tiled=True)
    stats = got[:, ROWS:].reshape(8, 2, 4, 128)
    stats = stats.transpose(0, 2, 1, 3).reshape(8, 4, ROWS)
    sums = []
    for k in (0, 2):
        tops = stats[:, k]
        top = jnp.max(tops, axis=0)
        shares = jnp.exp(tops - top[None])
        total = jnp.sum(shares * stats[:, k + 1], axis=0)
        shares = shares / total[None]
        lanes = slice(0, COLS) if k == 0 else slice(COLS, 2 * COLS)
        sums.append(jnp.sum(got[:, :ROWS, lanes] * shares[:, :, None], axis=0))
    gap_text = sums[0] - sums[1]

    piece = jnp.concatenate([gap_text[: ROWS // 2], gap_text[ROWS // 2 :]], axis=1)
    term = halved(dot(gap_text, image_student, ((0,), (0,))), starts, CORE)
    for pairs in (X_FLIP, Z_FOLD[0]):
        term = term + move(term, pairs)
    halves = [term[: SHARD // 2], term[SHARD // 2 :]]
    halves = [half + move(half, pairs) for half, pairs in zip(halves, Z_FOLD[1:])]
    received = [move(half, pairs) for half, pairs in zip(halves, Z_FOLD[:0:-1])]
    packed = pack(piece, jnp.concatenate(halves), jnp.concatenate(received), scale_s / math.sqrt(batch))

    pieces = lax.all_to_all(packed, ("xl", "y"), 0, 0, tiled=True)
    partner = move(pieces[:, ROWS // 2 :], CORE)
    where = jnp.stack([xh, core]).astype(jnp.int32)
    return unpack_image(where, pieces, head, scale_s), unpack_head(where, pieces, partner)


def solution(mesh):
    fine = Mesh(mesh.devices.reshape(SIZES), AXES)
    dp, every = ("z", "xh", "core"), AXES
    in_specs = (P(dp, None), P(dp, None), P(every, None), P(every, None), P())
    out_specs = (P(dp, None), P())
    return jax.shard_map(shards, mesh=fine, in_specs=in_specs, out_specs=out_specs, check_vma=False)
```

```python
import math

import jax
import jax.numpy as jnp
from jax import lax
from jax.experimental import pallas as pl
from jax.experimental.pallas import tpu as pltpu
from jax.sharding import Mesh, PartitionSpec as P

AXES = ("z", "xh", "core", "xl", "y")
SIZES = (8, 2, 2, 2, 4)
HIGH = lax.Precision.HIGH
DS, DT = 512, 768
ROWS = 256
SHARD = 32
COLS = DS // 8
VMEM_LIMIT = 14 * 1024 * 1024


def linear(z, xh, core, xl, y):
    return (((z * 2 + xh) * 2 + core) * 2 + xl) * 4 + y


def moves(place):
    pairs = []
    for z in range(8):
        for xh in range(2):
            for core in range(2):
                for xl in range(2):
                    for y in range(4):
                        here = (z, xh, core, xl, y)
                        pairs.append((linear(*here), linear(*place(*here))))
    return pairs


Z_NEXT = moves(lambda z, xh, core, xl, y: ((z + 1 - 2 * core) % 8, xh, core, xl, y))
X_FLIP = moves(lambda z, xh, core, xl, y: (z, 1 - xh, core, 1 - xl, y))
CORE = moves(lambda z, xh, core, xl, y: (z, xh, 1 - core, xl, y))
Z_FOLD = tuple(
    moves(lambda z, xh, core, xl, y, bit=bit: (z ^ bit, xh, core, xl, y)) for bit in (1, 2, 6)
)


def move(array, pairs):
    return lax.ppermute(array, AXES, pairs)


def dot(a, b, dims):
    return lax.dot_general(
        a, b, (dims, ((), ())), precision=HIGH, preferred_element_type=jnp.float32
    )


def split(x):
    high = x.astype(jnp.bfloat16)
    return high, (x - high.astype(jnp.float32)).astype(jnp.bfloat16)


def dot3(a, b, dims):
    def one(p, q):
        return lax.dot_general(p, q, (dims, ((), ())), preferred_element_type=jnp.float32)

    return one(a[0], b[0]) + (one(a[0], b[1]) + one(a[1], b[0]))


NT = ((1,), (1,))
NN = ((1,), (0,))


def texts_kernel(count, first, last, *refs):
    refs = list(refs)
    place = refs.pop(0) if last else None
    folded_ref, images_ref = refs.pop(0), refs.pop(0)
    arrays = [refs.pop(0) for _ in range(count)]
    state = None if first else [refs.pop(0) for _ in range(3)]
    outs = [refs.pop(0) for _ in range(1 if last else 3)]
    t_high, t_low, f_high, f_low = refs
    start = 0
    for array in arrays:
        here = pl.ds(start, array.shape[0])
        start += array.shape[0]
        t_high[here, :], t_low[here, :] = split(array[:, :DT])
        f_high[here, :], f_low[here, :] = split(array[:, DT:])
    texts = (t_high[...], t_low[...])
    features = (f_high[...], f_low[...])
    tiles = (
        dot3(split(folded_ref[...]), features, NT),
        dot3(split(images_ref[...]), texts, NT),
    )
    lane = lax.broadcasted_iota(jnp.int32, (ROWS, 128), 1)
    stats = jnp.zeros((ROWS, 128), jnp.float32)
    products = []
    for k, tile in enumerate(tiles):
        top = jnp.max(tile, axis=1, keepdims=True)
        if not first:
            old_top = state[0][:, 2 * k : 2 * k + 1]
            top = jnp.maximum(top, old_top)
        weight = jnp.exp(tile - top)
        total = jnp.sum(weight, axis=1, keepdims=True)
        product = dot3(split(weight), features, NN)
        if not first:
            shrink = jnp.exp(old_top - top)
            total = total + shrink * state[0][:, 2 * k + 1 : 2 * k + 2]
            product = product + shrink * state[1 + k][...]
        stats = jnp.where(lane == 2 * k, top, stats)
        stats = jnp.where(lane == 2 * k + 1, total, stats)
        products.append(product)
    if not last:
        outs[0][...] = stats
        outs[1][...] = products[0]
        outs[2][...] = products[1]
        return
    out = outs[0]
    turned = stats.T[:8]
    for q in range(4):
        a = products[0][:, 128 * q : 128 * q + 128]
        b = products[1][:, 128 * q : 128 * q + 128]
        out[place[2 * q], 0:ROWS] = jnp.where(lane < COLS, a, pltpu.roll(b, COLS, 1))
        out[place[2 * q + 1], 0:ROWS] = jnp.where(lane < COLS, pltpu.roll(a, COLS, 1), b)
    for k in range(8):
        out[k, ROWS : ROWS + 4] = turned[:4, :128]
        out[k, ROWS + 4 : ROWS + 8] = turned[:4, 128:]


def add_texts(folded, images, arrays, state=None, place=None):
    first, last = state is None, place is not None
    texts = sum(array.shape[0] for array in arrays)
    operands = [folded, images] + list(arrays) + ([] if first else list(state))
    vmem = pl.BlockSpec(memory_space=pltpu.VMEM)
    in_specs = [vmem] * len(operands)
    scratch = [
        pltpu.VMEM((texts, DT), jnp.bfloat16),
        pltpu.VMEM((texts, DT), jnp.bfloat16),
        pltpu.VMEM((texts, DS), jnp.bfloat16),
        pltpu.VMEM((texts, DS), jnp.bfloat16),
    ]
    if last:
        operands = [place] + operands
        in_specs = [pl.BlockSpec(memory_space=pltpu.SMEM)] + in_specs
        shapes = [jax.ShapeDtypeStruct((8, ROWS + 8, 128), jnp.float32)]
    else:
        shapes = [
            jax.ShapeDtypeStruct((ROWS, 128), jnp.float32),
            jax.ShapeDtypeStruct((ROWS, DS), jnp.float32),
            jax.ShapeDtypeStruct((ROWS, DS), jnp.float32),
        ]
    flops = 2 * 3 * ROWS * texts * (DT + 3 * DS)

    def body(*refs):
        texts_kernel(len(arrays), first, last, *refs)

    return pl.pallas_call(
        body,
        out_shape=shapes,
        in_specs=in_specs,
        out_specs=[vmem] * len(shapes),
        scratch_shapes=scratch,
        compiler_params=pltpu.CompilerParams(vmem_limit_bytes=VMEM_LIMIT),
        cost_estimate=pl.CostEstimate(
            flops=40 * flops, bytes_accessed=4 * 1024 * 1024, transcendentals=2 * ROWS * texts
        ),
        name="add_texts",
    )(*operands)


def halved(array, starts, pairs):
    shape = (array.shape[0] // 2, array.shape[1])
    mine, other = [lax.dynamic_slice(array, (at, jnp.uint32(0)), shape) for at in starts]
    return mine + move(other, pairs)


def small_call(body, shape, *operands, scalars=0):
    smem, vmem = pl.BlockSpec(memory_space=pltpu.SMEM), pl.BlockSpec(memory_space=pltpu.VMEM)
    return pl.pallas_call(
        body,
        out_shape=jax.ShapeDtypeStruct(shape, jnp.float32),
        in_specs=[smem] * scalars + [vmem] * (len(operands) - scalars),
        out_specs=vmem,
        compiler_params=pltpu.CompilerParams(vmem_limit_bytes=VMEM_LIMIT),
        cost_estimate=pl.CostEstimate(flops=1024, bytes_accessed=1024 * 1024, transcendentals=0),
    )(*operands)


def pack(piece, term, received, scale):
    def body(piece_ref, term_ref, received_ref, out):
        total = scale * (term_ref[...] + received_ref[...])
        for k in range(8):
            out[k, : ROWS // 2] = piece_ref[...]
            for q in range(4):
                here = slice(ROWS // 2 + SHARD * q, ROWS // 2 + SHARD * (q + 1))
                out[k, here] = total[:, 128 * q : 128 * (q + 1)]

    return small_call(body, (8, ROWS, 128), piece, term, received)


def unpack_image(where, pieces, head, scale):
    def body(where_ref, pieces_ref, head_ref, out):
        lane = lax.broadcasted_iota(jnp.int32, (ROWS // 2, 128), 1)
        total = jnp.zeros((ROWS, DS), jnp.float32)
        for half in (0, 1):
            columns = []
            for q in (2 * half, 2 * half + 1):
                a, b = pieces_ref[2 * q, : ROWS // 2], pieces_ref[2 * q + 1, : ROWS // 2]
                top = jnp.where(lane < COLS, a, pltpu.roll(b, COLS, 1))
                bottom = jnp.where(lane < COLS, pltpu.roll(a, COLS, 1), b)
                columns.append(jnp.concatenate([top, bottom], axis=0))
            gap = jnp.concatenate(columns, axis=1)
            start = pl.multiple_of((DS // 2) * lax.rem(where_ref[0] + half, 2), DS // 2)
            total += dot3(split(gap), split(head_ref[pl.ds(start, DS // 2), :]), NN)
        out[...] = scale * total

    return small_call(body, (ROWS, DS), where, pieces, head, scalars=1)


def unpack_head(where, pieces, partner):
    def body(where_ref, pieces_ref, partner_ref, out):
        core = where_ref[1]
        for i in range(4):
            k = lax.rem(4 * (pl.program_id(0) + where_ref[0]) + i, 8)
            mine = pl.multiple_of(i * COLS + core * SHARD, SHARD)
            other = pl.multiple_of(i * COLS + (1 - core) * SHARD, SHARD)
            for q in range(4):
                lanes = slice(128 * q, 128 * (q + 1))
                here = slice(ROWS // 2 + SHARD * q, ROWS // 2 + SHARD * (q + 1))
                out[pl.ds(mine, SHARD), lanes] = pieces_ref[k, here]
                out[pl.ds(other, SHARD), lanes] = partner_ref[k, SHARD * q : SHARD * (q + 1)]

    vmem = pl.BlockSpec(memory_space=pltpu.VMEM)
    return pl.pallas_call(
        body,
        out_shape=jax.ShapeDtypeStruct((DS, DS), jnp.float32),
        grid=(2,),
        in_specs=[pl.BlockSpec(memory_space=pltpu.SMEM), vmem, vmem],
        out_specs=pl.BlockSpec((DS // 2, DS), lambda i: (i, 0)),
        compiler_params=pltpu.CompilerParams(vmem_limit_bytes=VMEM_LIMIT),
        cost_estimate=pl.CostEstimate(flops=1024, bytes_accessed=1024 * 1024, transcendentals=0),
    )(where, pieces, partner)


def shards(image_student, image_teacher, text_features, text_teacher, head):
    scale_s = 4.0 / math.sqrt(DS)
    scale_t = 4.0 / math.sqrt(DT)
    batch = ROWS * 32
    xh, core = lax.axis_index("xh"), lax.axis_index("core")

    own = [text_teacher, text_features]
    near = [move(array, CORE) for array in own]
    far = [move(array, X_FLIP) for array in own]
    one = jnp.concatenate([jnp.concatenate(part, axis=1) for part in (own, near)], axis=0)
    *far, _ = lax.optimization_barrier((*far, one))
    last = [move(array, CORE) for array in far]
    two = jnp.concatenate([jnp.concatenate(part, axis=1) for part in (far, last)], axis=0)
    students, _ = lax.optimization_barrier((image_student, one))
    folded = scale_s * dot(students, head, NT)
    images = scale_t * image_teacher
    state = add_texts(folded, images, [one, two])
    for step in range(3):
        one, two = move(one, Z_NEXT), move(two, Z_NEXT)
        state = add_texts(folded, images, [one, move(one, CORE)], state)
        if step == 2:
            one = move(one[:SHARD], Z_NEXT)
            one, *state = lax.optimization_barrier((one, *state))
        state = add_texts(folded, images, [two, move(two, CORE)], state)
    two = move(two[:SHARD], Z_NEXT)
    two, *state = lax.optimization_barrier((two, *state))
    state = add_texts(folded, images, [one, move(one, CORE)], state)
    place = jnp.arange(8, dtype=jnp.int32) ^ (4 * xh).astype(jnp.int32)
    (both,) = add_texts(folded, images, [two, move(two, CORE)], state, place)

    starts = [(core * SHARD).astype(jnp.uint32), ((1 - core) * SHARD).astype(jnp.uint32)]
    both, *starts = lax.optimization_barrier((both, *starts))
    got = lax.all_to_all(both, ("xl", "y"), 0, 0, tiled=True)
    stats = got[:, ROWS:].reshape(8, 2, 4, 128)
    stats = stats.transpose(0, 2, 1, 3).reshape(8, 4, ROWS)
    sums = []
    for k in (0, 2):
        tops = stats[:, k]
        top = jnp.max(tops, axis=0)
        shares = jnp.exp(tops - top[None])
        total = jnp.sum(shares * stats[:, k + 1], axis=0)
        shares = shares / total[None]
        lanes = slice(0, COLS) if k == 0 else slice(COLS, 2 * COLS)
        sums.append(jnp.sum(got[:, :ROWS, lanes] * shares[:, :, None], axis=0))
    gap_text = sums[0] - sums[1]

    piece = jnp.concatenate([gap_text[: ROWS // 2], gap_text[ROWS // 2 :]], axis=1)
    term = halved(dot(gap_text, image_student, ((0,), (0,))), starts, CORE)
    for pairs in (X_FLIP,) + Z_FOLD[:-1]:
        term = term + move(term, pairs)
    packed = pack(piece, term, move(term, Z_FOLD[-1]), scale_s / math.sqrt(batch))

    pieces = lax.all_to_all(packed, ("xl", "y"), 0, 0, tiled=True)
    partner = move(pieces[:, ROWS // 2 :], CORE)
    where = jnp.stack([xh, core]).astype(jnp.int32)
    return unpack_image(where, pieces, head, scale_s), unpack_head(where, pieces, partner)


def solution(mesh):
    fine = Mesh(mesh.devices.reshape(SIZES), AXES)
    dp, every = ("z", "xh", "core"), AXES
    in_specs = (P(dp, None), P(dp, None), P(every, None), P(every, None), P())
    out_specs = (P(dp, None), P())
    return jax.shard_map(shards, mesh=fine, in_specs=in_specs, out_specs=out_specs, check_vma=False)
```
